32 devices in a mesh: expert: 4 (over y, x), seq: 8 (over z, core).
Axes of the slice: x: 2, y: 2, z: 4, core: 2. Of those that a mesh axis runs over, the one named last changes fastest.
Arguments:
- moe_input: bfloat16 [8, 256, 2048], P('seq', 'expert'), may hold values from -6 to 6
- out_grad: bfloat16 [8, 256, 2048], P('seq', 'expert'), may hold values from -6 to 6
- expert_id: int32 [8, 256, 1], P('seq', 'expert'), may hold values from 0 to 7; in each aligned block of 64 rows (0 to 63, 64 to 127, ..., all dimensions but the last counted through in order) at most 10 rows name the same one
- w_gate: bfloat16 [8, 2048, 8192], P('expert', None, 'seq'), may hold values from -0.125 to 0.125
- w_up: bfloat16 [8, 2048, 8192], P('expert', None, 'seq'), may hold values from -0.125 to 0.125
- w_down: bfloat16 [8, 8192, 2048], P('expert', 'seq'), may hold values from -0.0625 to 0.0625
- w_out: bfloat16 [4096, 2048], P('expert'), may hold values from -0.09375 to 0.09375
- b_proj: bfloat16 [8, 256, 128], P('seq'), may hold values from -6 to 6
- c_proj: bfloat16 [8, 256, 128], P('seq'), may hold values from -0.046875 to 0.046875
- log_decay: float32 [8, 64, 256], P('seq', 'expert'), may hold values from -0.7 to 0, as said below
Outputs:
- head_grad: bfloat16 [8, 256, 4096], P('seq', None, 'expert')
- input_grad: bfloat16 [8, 256, 2048], P('seq', 'expert')
- gate_grad: float32 [8, 2048, 8192], P('expert', None, 'seq')
- up_grad: float32 [8, 2048, 8192], P('expert', None, 'seq')
- down_grad: float32 [8, 8192, 2048], P('expert', 'seq')
The draws below stay inside these ranges and needn't reach their ends.
Inputs may be any that keep to these rules, and one draw needn't show every extreme that they name: `expert_id`: at most 10 tokens of one aligned block of 64 tokens (one device's tokens) name the same expert, and some block reaches 10. `log_decay`: Negative.
All inputs are finite; a program needn't handle non-finite values.
Results may differ from the reference program's by a relative error of at most 0.019.
Values may be sent and summed in bfloat16 or wider, within the bound.
A program may use at most 192 MiB of HBM per device.

```python
import math
import jax
import jax.numpy as jnp
import numpy as np
from jax import lax

D = 2048
FF = 8192
RECURRENT_LANES = 64
P_SIZE = 64
N = 128
TOK_DEV = 64
CAP = 10
PIECE_LENGTH = 256
SPAN_PARTITIONS = 8
EXPERTS = 8
TOKENS = 2048
N_EXPERT = 4
N_SEQ = 8


def draw_log_decay(key, part):
    streams = jax.random.split(key, 7)
    total = SPAN_PARTITIONS * PIECE_LENGTH
    fast_share = 0.5
    fast = jax.random.uniform(streams[0], (1, RECURRENT_LANES, 1)) < fast_share
    fast_rate = jax.random.uniform(streams[1], (1, RECURRENT_LANES, 1), minval=1.0 / 50.0, maxval=1.0 / 30.0)
    slow_rate = jax.random.uniform(streams[2], (1, RECURRENT_LANES, 1), minval=0.15, maxval=0.6) / total
    device_factor = jnp.exp(jax.random.uniform(streams[3], (SPAN_PARTITIONS, RECURRENT_LANES, 1), minval=-0.35, maxval=0.35))
    token_factor = jax.random.uniform(streams[4], (SPAN_PARTITIONS, RECURRENT_LANES, PIECE_LENGTH), minval=0.5, maxval=1.5)
    fading_speeds = jnp.where(fast, fast_rate, slow_rate) * device_factor * token_factor
    expert_locations = jax.random.randint(streams[5], (2,), 0, total)
    surviving_entries = jax.random.uniform(streams[6], (2, RECURRENT_LANES), minval=0.55, maxval=0.8)
    element_offset = (jnp.arange(SPAN_PARTITIONS)[:, None] * PIECE_LENGTH + jnp.arange(PIECE_LENGTH)[None, :])[:, None, :]
    spike_occurrences = jnp.zeros((SPAN_PARTITIONS, RECURRENT_LANES, PIECE_LENGTH), jnp.float32)
    for chosen_expert_number in range(2):
        spike_occurrences = spike_occurrences + jnp.where(element_offset == expert_locations[chosen_expert_number], jnp.log(surviving_entries[chosen_expert_number])[None, :, None], 0.0)
    return (spike_occurrences - fading_speeds).astype(jnp.float32)


def block_levels(key, extent, cuts, smallest, top_value):
    loudness, own = 1.0, jax.random.fold_in(key, 6)
    for axis_at, blocks in cuts:
        steps = jnp.exp(jax.random.uniform(jax.random.fold_in(own, axis_at), (blocks,), jnp.float32, smallest / len(cuts), top_value / len(cuts)))
        loudness = loudness * jnp.repeat(steps, extent[axis_at] // blocks).reshape([-1 if axis == axis_at else 1 for axis in range(len(extent))])
    return loudness


def deal_out(rng, own, number, rows, number_of, top, bound, lean):
    sequence = jax.random.permutation(rng, number_of)
    heavy_load, ordinary = shares(number_of, rows * top, bound, lean, True), shares(number_of, rows * top, bound, lean, False)
    places = jnp.arange(number_of)

    def named(lengths, turn):
        used = int((lengths > 0).sum())
        fixed = max(1, used // 4)
        passed = fixed + (places - fixed + turn * (used - fixed)) % max(1, number_of - fixed)
        return jnp.zeros((number_of,), jnp.int32).at[sequence[jnp.where(places < fixed, places, passed)]].set(jnp.asarray(lengths, jnp.int32))

    lengths = jnp.where(number % 4 == 0, named(heavy_load, number // 4), named(ordinary, number - number // 4 - 1))
    mixed = jax.random.permutation(jax.random.fold_in(own, 3), number_of)
    donor, taker = mixed[0:number_of // 2 * 2:2], mixed[1:number_of // 2 * 2:2]
    margin = jnp.minimum(lengths[donor] - 1, bound - lengths[taker]) // 2
    margin = jnp.where((donor == sequence[0]) | (taker == sequence[0]) | (lengths[taker] == 0), 0, jnp.maximum(margin, 0))
    passed = jax.random.randint(jax.random.fold_in(own, 4), (number_of // 2,), 0, 1 << 20) % (margin + 1)
    lengths = lengths.at[donor].add(-passed).at[taker].add(passed)
    items = jnp.searchsorted(jnp.cumsum(lengths), jnp.arange(rows * top), side="right").astype(jnp.int32)
    listing = items.reshape(top, rows).T
    listing = listing[jax.random.permutation(jax.random.fold_in(own, 1), rows)]
    turn = jax.random.randint(jax.random.fold_in(own, 2), (rows, 1), 0, top)
    return jnp.take_along_axis(listing, (jnp.arange(top)[None, :] + turn) % top, axis=1)


def shares(number_of, total, limit, lean, full):
    loads = [(1 << 20) // math.isqrt(rank ** lean) + 1 for rank in range(1, number_of + 1)]
    largest = limit if full else min(limit, max(-(-total // number_of), total * loads[0] // sum(loads)))
    least = 1 if total - largest >= number_of - 1 else 0
    given, rest = [largest] + [least] * (number_of - 1), total - largest - least * (number_of - 1)
    while rest > 0:
        movable = [i for i in range(1, number_of) if given[i] < largest] or [i for i in range(1, number_of) if given[i] < limit]
        whole, remaining = sum([loads[i] for i in movable]), rest
        for i in movable:
            more = min(limit - given[i], max(1, remaining * loads[i] // whole), rest)
            given[i] = given[i] + more
            rest = rest - more
    return np.array(given)


def centred(own_key, shape, scale, limit, cuts=(), kind=jnp.bfloat16):
    array = scale * jax.random.normal(own_key, shape, jnp.float32)
    if cuts:
        array = array * block_levels(own_key, shape, cuts, -0.22, 0.18)
    return jnp.clip(array, -limit, limit).astype(kind)


def setup_inputs(seed: int = 0) -> dict:
    key_of = jax.random.split(jax.random.key(seed), 11)
    moe_input = centred(key_of[0], (SPAN_PARTITIONS, PIECE_LENGTH, D), 1.0, 6.0, ((0, 8), (1, 4)))
    out_grad = centred(key_of[1], (SPAN_PARTITIONS, PIECE_LENGTH, D), 1.0, 6.0, ((0, 8), (1, 4)))
    expert_id_keys = jax.random.split(jax.random.fold_in(key_of[2], 1), SPAN_PARTITIONS * PIECE_LENGTH // TOK_DEV)
    expert_id_turns = jax.random.permutation(jax.random.fold_in(key_of[2], 3), SPAN_PARTITIONS * PIECE_LENGTH // TOK_DEV)
    expert_id = jax.vmap(lambda own, number: deal_out(jax.random.fold_in(key_of[2], 2), own, number, TOK_DEV, EXPERTS, 1, CAP, 1))(expert_id_keys, expert_id_turns).reshape((SPAN_PARTITIONS, PIECE_LENGTH, 1))
    w_gate = centred(key_of[3], (EXPERTS, D, FF), D ** -0.5, 0.125, ((0, 4), (2, 8)))
    w_up = centred(key_of[4], (EXPERTS, D, FF), D ** -0.5, 0.125, ((0, 4), (2, 8)))
    w_down = centred(key_of[5], (EXPERTS, FF, D), FF ** -0.5, 0.0625, ((0, 4), (1, 8)))
    w_out = centred(key_of[6], (RECURRENT_LANES * P_SIZE, D), (RECURRENT_LANES * P_SIZE) ** -0.5, 0.09375, ((0, 4),))
    b_proj = centred(key_of[7], (SPAN_PARTITIONS, PIECE_LENGTH, N), 1.0, 6.0, ((0, 8),))
    c_proj = centred(key_of[8], (SPAN_PARTITIONS, PIECE_LENGTH, N), 0.003, 0.046875, ((0, 8),))
    log_decay = draw_log_decay(jax.random.fold_in(key_of[10], 71), 0)
    return dict(moe_input=moe_input, out_grad=out_grad, expert_id=expert_id, w_gate=w_gate, w_up=w_up, w_down=w_down, w_out=w_out, b_proj=b_proj, c_proj=c_proj, log_decay=log_decay)


def silu_parts(gate):
    logistic = jax.nn.sigmoid(gate)
    return (gate * logistic, logistic)

def shard_grad(decay, b_rows, c_rows, head_rows, carried):
    length = b_rows.shape[0]
    acum = jnp.cumsum(decay, axis=1)
    later = jnp.arange(length, dtype=jnp.int32)[:, None] >= jnp.arange(length, dtype=jnp.int32)[None, :]
    scores = lax.dot_general(c_rows, b_rows, (((1,), (1,)), ((), ())), preferred_element_type=jnp.float32)
    spread = acum[:, :, None] - acum[:, None, :]
    weight = jnp.where(later[None], jnp.exp(jnp.where(later[None], spread, 0.0)), 0.0) * scores[None]
    local = jnp.einsum('hts,thp->shp', weight, head_rows, precision=lax.Precision.HIGHEST)
    tail = jnp.exp(acum[:, -1:] - acum)
    cross = jnp.einsum('hs,sn,hnp->shp', tail, b_rows.astype(jnp.float32), carried, precision=lax.Precision.HIGHEST)
    weighted = jnp.exp(acum)
    summary = jnp.einsum('ht,tn,thp->hnp', weighted, c_rows.astype(jnp.float32), head_rows, precision=lax.Precision.HIGHEST)
    return (local + cross, summary, weighted[:, -1])

def reference(moe_input, out_grad, expert_id, w_gate, w_up, w_down, w_out, b_proj, c_proj, log_decay):
    blocks = SPAN_PARTITIONS * N_EXPERT
    rows = blocks * CAP
    slice_width = FF // N_SEQ
    flat_x = moe_input.reshape(blocks, TOK_DEV, D)
    flat_dy = out_grad.reshape(blocks, TOK_DEV, D)
    labels = expert_id.reshape(blocks, TOK_DEV)
    onehot = (labels[:, :, None] == jnp.arange(EXPERTS, dtype=jnp.int32)[None, None, :]).astype(jnp.int32)
    slot_index = lax.optimization_barrier(jnp.sum((jnp.cumsum(onehot, axis=1) - onehot) * onehot, axis=2))
    buffer_row = (jnp.arange(blocks, dtype=jnp.int32)[:, None] * CAP + slot_index).astype(jnp.int32)
    x_buffer = jnp.zeros((EXPERTS, rows, D), jnp.bfloat16).at[labels, buffer_row].set(flat_x)
    dy_buffer = jnp.zeros((EXPERTS, rows, D), jnp.bfloat16).at[labels, buffer_row].set(flat_dy)

    def one_expert(operands):
        x_rows, dy_rows, wg, wu, wd = operands
        gate = jnp.dot(x_rows, wg, preferred_element_type=jnp.float32)
        up = jnp.dot(x_rows, wu, preferred_element_type=jnp.float32)
        activated, logistic = silu_parts(gate)
        hidden = (activated * up).astype(jnp.bfloat16)
        hidden_grad = lax.dot_general(dy_rows, wd, (((1,), (1,)), ((), ())), preferred_element_type=jnp.float32)
        up_term = (hidden_grad * activated).astype(jnp.bfloat16)
        gate_term = (hidden_grad * up * logistic * (1.0 + gate * (1.0 - logistic))).astype(jnp.bfloat16)
        grad_g = lax.dot_general(x_rows, gate_term, (((0,), (0,)), ((), ())), preferred_element_type=jnp.float32)
        grad_u = lax.dot_general(x_rows, up_term, (((0,), (0,)), ((), ())), preferred_element_type=jnp.float32)
        grad_d = lax.dot_general(hidden, dy_rows, (((0,), (0,)), ((), ())), preferred_element_type=jnp.float32)
        gate_slices = gate_term.reshape(rows, N_SEQ, slice_width).transpose(1, 0, 2)
        up_slices = up_term.reshape(rows, N_SEQ, slice_width).transpose(1, 0, 2)
        wg_slices = wg.reshape(D, N_SEQ, slice_width).transpose(1, 0, 2)
        wu_slices = wu.reshape(D, N_SEQ, slice_width).transpose(1, 0, 2)

        def add_slice(total, pieces):
            g_part, u_part, wg_part, wu_part = pieces
            partial_sum = lax.dot_general(g_part, wg_part, (((1,), (1,)), ((), ())), preferred_element_type=jnp.float32)
            partial_sum = partial_sum + lax.dot_general(u_part, wu_part, (((1,), (1,)), ((), ())), preferred_element_type=jnp.float32)
            rounded = lax.optimization_barrier(partial_sum.astype(jnp.bfloat16))
            return (total + rounded.astype(jnp.float32), None)
        back_sum, _ = lax.scan(add_slice, jnp.zeros((rows, D), jnp.float32), (gate_slices, up_slices, wg_slices, wu_slices))
        return (back_sum.astype(jnp.bfloat16), grad_g, grad_u, grad_d)
    back_rows, gate_grad, up_grad, down_grad = lax.map(one_expert, (x_buffer, dy_buffer, w_gate, w_up, w_down))
    expert_grad = back_rows[labels, buffer_row]
    input_grad = (flat_dy.astype(jnp.float32) + expert_grad.astype(jnp.float32)).astype(jnp.bfloat16)
    grads_flat = out_grad.reshape(TOKENS, D)
    expert_flat = expert_grad.reshape(TOKENS, D)
    head_out = lax.dot_general(grads_flat, w_out, (((1,), (1,)), ((), ())), preferred_element_type=jnp.float32)
    head_out = head_out + lax.dot_general(expert_flat, w_out, (((1,), (1,)), ((), ())), preferred_element_type=jnp.float32)
    head_out = head_out.reshape(SPAN_PARTITIONS, PIECE_LENGTH, RECURRENT_LANES, P_SIZE)

    def shard_step(carried, pieces):
        decay, b_rows, c_rows, head_rows = pieces
        result, summary, total = shard_grad(decay, b_rows, c_rows, head_rows, carried)
        new_state = summary + total[:, None, None] * carried
        return (new_state, result.astype(jnp.bfloat16))
    _, head_grad = lax.scan(shard_step, jnp.zeros((RECURRENT_LANES, N, P_SIZE), jnp.float32), (log_decay, b_proj, c_proj, head_out), reverse=True)
    head_grad = head_grad.reshape(SPAN_PARTITIONS, PIECE_LENGTH, RECURRENT_LANES * P_SIZE)
    return (head_grad, input_grad.reshape(SPAN_PARTITIONS, PIECE_LENGTH, D), gate_grad, up_grad, down_grad)
```

```python
import jax
import jax.numpy as jnp
from jax import lax
from jax.experimental import pallas as pl
from jax.experimental.pallas import tpu as pltpu
from jax.sharding import PartitionSpec as P

P_SIZE = 64
CAP = 10
VMEM = 60 * 1024 * 1024
NN = (((1,), (0,)), ((), ()))
NT = (((1,), (1,)), ((), ()))
TN = (((0,), (0,)), ((), ()))


def mm(a, b, dims):
    return lax.dot_general(a, b, dims, preferred_element_type=jnp.float32)


def terms_kernel(x_ref, dy_ref, wg_ref, wu_ref, wd_ref, h_ref, g_ref, u_ref, back_ref, acc):
    step = pl.program_id(0)
    x = x_ref[...]
    gate = mm(x, wg_ref[0], NN)
    up = mm(x, wu_ref[0], NN)
    grad = mm(dy_ref[...], wd_ref[0], NT)
    logistic = jax.nn.sigmoid(gate)
    activated = gate * logistic
    h_ref[...] = (activated * up).astype(jnp.bfloat16)
    up_term = (grad * activated).astype(jnp.bfloat16)
    gate_term = (grad * up * logistic * (1.0 + gate * (1.0 - logistic))).astype(jnp.bfloat16)
    g_ref[...] = gate_term
    u_ref[...] = up_term
    part = mm(gate_term, wg_ref[0], NT) + mm(up_term, wu_ref[0], NT)

    @pl.when(step == 0)
    def _():
        acc[...] = part

    @pl.when(step > 0)
    def _():
        acc[...] += part

    @pl.when(step == pl.num_programs(0) - 1)
    def _():
        back_ref[...] = acc[...].astype(jnp.bfloat16)


def expert_terms(e, x, dy, w_gate, w_up, w_down):
    rows, width = x.shape
    hidden = w_gate.shape[2]
    tile = min(256, hidden)
    whole = pl.BlockSpec((rows, width), lambda i: (0, 0))
    part = pl.BlockSpec((rows, tile), lambda i: (0, i))
    column = pl.BlockSpec((1, width, tile), lambda i: (e, 0, i))
    row = pl.BlockSpec((1, tile, width), lambda i: (e, i, 0))
    term = jax.ShapeDtypeStruct((rows, hidden), jnp.bfloat16)
    return pl.pallas_call(
        terms_kernel,
        grid=(hidden // tile,),
        in_specs=[whole, whole, column, column, row],
        out_specs=[part, part, part, whole],
        out_shape=[term, term, term, jax.ShapeDtypeStruct((rows, width), jnp.bfloat16)],
        scratch_shapes=[pltpu.VMEM((rows, width), jnp.float32)],
        compiler_params=pltpu.CompilerParams(vmem_limit_bytes=VMEM),
        cost_estimate=pl.CostEstimate(
            flops=10 * rows * width * hidden,
            bytes_accessed=6 * width * hidden + 6 * rows * width,
            transcendentals=rows * hidden,
        ),
        name="expert_terms",
    )(x, dy, w_gate, w_up, w_down)


def weight_grads(e, count, left, rights, held):
    rows, width = left.shape
    breadth = rights[0].shape[1]
    tile = min(256, width)
    number = len(rights)

    def kernel(*refs):
        left_ref, right_refs, out_refs = refs[0], refs[1 : 1 + number], refs[-number:]
        for right_ref, out_ref in zip(right_refs, out_refs):
            out_ref[0] = mm(left_ref[...], right_ref[...], TN)

    out = pl.BlockSpec((1, tile, breadth), lambda i: (e, i, 0))
    kept = [] if held is None else list(held)
    return pl.pallas_call(
        kernel,
        grid=(width // tile,),
        in_specs=[pl.BlockSpec((rows, tile), lambda i: (0, i))]
        + [pl.BlockSpec((rows, breadth), lambda i: (0, 0))] * number
        + [pl.BlockSpec(memory_space=pl.ANY)] * len(kept),
        out_specs=[out] * number,
        out_shape=[jax.ShapeDtypeStruct((count, width, breadth), jnp.float32)] * number,
        input_output_aliases={1 + number + k: k for k in range(len(kept))},
        compiler_params=pltpu.CompilerParams(vmem_limit_bytes=VMEM),
        cost_estimate=pl.CostEstimate(
            flops=2 * number * rows * width * breadth,
            bytes_accessed=4 * number * width * breadth,
            transcendentals=0,
        ),
        name="weight_grads",
    )(left, *rights, *kept)


def body(moe_input, out_grad, expert_id, w_gate, w_up, w_down, w_out, b_proj, c_proj, log_decay):
    groups = lax.axis_size("expert")
    group = lax.axis_index("expert")
    shards = lax.axis_size("seq")
    shard = lax.axis_index("seq")
    local = w_gate.shape[0]
    tokens, width = moe_input.shape[1:]
    heads = w_out.shape[0] // P_SIZE
    lanes = heads * P_SIZE
    length, state = b_proj.shape[1:]
    bf = jnp.bfloat16

    labelled = jnp.concatenate(
        [moe_input[0], jnp.broadcast_to(expert_id[0], (tokens, 128)).astype(bf)], axis=1
    )
    x_all = lax.all_gather(labelled, "expert", axis=0, tiled=True)
    dy_all = lax.all_gather(out_grad[0], "expert", axis=0, tiled=True)
    labels = x_all[:, width].astype(jnp.int32)
    x_all = x_all[:, :width]
    here = jnp.arange(length, dtype=jnp.int32)
    same = (
        (labels[:, None] == labels[None, :])
        & (here[:, None] // tokens == here[None, :] // tokens)
        & (here[None, :] < here[:, None])
    )
    slot = jnp.sum(same.astype(jnp.int32), axis=1)
    place = (here // tokens) * CAP + slot
    span = groups * CAP

    xs, dys = [], []
    for e in range(local):
        mine = jnp.where(labels == group * local + e, place, -1)
        pick = (jnp.arange(span, dtype=jnp.int32)[:, None] == mine[None, :]).astype(bf)
        xs.append(mm(pick, x_all, NN).astype(bf))
        dys.append(mm(pick, dy_all, NN).astype(bf))
    gathered = [
        [lax.all_gather(part, "seq", axis=0, tiled=True) for part in (xs[e], dys[e])]
        for e in range(local)
    ]

    gate_up, down, returned = None, None, []
    for e in range(local):
        x, dy = gathered[e]
        hidden, gate_term, up_term, back = expert_terms(e, x, dy, w_gate, w_up, w_down)
        summed = lax.psum_scatter(back, "seq", scatter_dimension=0, tiled=True)
        returned.append(lax.all_gather(summed, "expert", axis=0, tiled=True))
        gate_up = weight_grads(e, local, x, [gate_term, up_term], gate_up)
        down = weight_grads(e, local, hidden, [dy], down)

    expert_all = 0.0
    for e in range(local):
        row = jnp.where(labels % local == e, (labels // local) * span + place, -1)
        take = (row[:, None] == jnp.arange(groups * span, dtype=jnp.int32)[None, :]).astype(bf)
        expert_all = expert_all + mm(take, returned[e], NN)
    expert_all = expert_all.astype(bf)
    own = lax.dynamic_slice_in_dim(expert_all, group * tokens, tokens, axis=0)
    input_grad = (out_grad[0].astype(jnp.float32) + own.astype(jnp.float32)).astype(bf)

    acum = jnp.cumsum(log_decay[0], axis=1)
    b_rows, c_rows = b_proj[0], c_proj[0]
    wide = jnp.repeat(acum.T, P_SIZE, axis=1)
    grow = jnp.exp(wide)
    tail = jnp.exp(wide[-1:] - wide)
    total = grow[-1:]
    high = total.astype(bf)
    low = (total - high.astype(jnp.float32)).astype(bf)
    later = here[:, None] >= here[None, :]
    scores = jnp.where(later, mm(c_rows, b_rows, NT), 0.0)
    difference = jnp.where(later[None], acum[:, :, None] - acum[:, None, :], 0.0)
    weight = (jnp.exp(difference) * scores[None]).astype(bf)

    head_out = mm(dy_all, w_out, NT) + mm(expert_all, w_out, NT)
    summary = mm(c_rows, (grow * head_out).astype(bf), TN).astype(bf)
    sent = jnp.concatenate([summary, high, low, jnp.zeros((14, lanes), bf)], axis=0)
    states = lax.all_gather(sent, "seq", axis=0, tiled=False)
    local_part = jnp.einsum(
        "hts,thp->shp",
        weight,
        head_out.astype(bf).reshape(length, heads, P_SIZE),
        preferred_element_type=jnp.float32,
    ).reshape(length, lanes)
    carried = jnp.zeros((state, lanes), jnp.float32)
    factor = jnp.ones((1, lanes), jnp.float32)
    for r in range(shards):
        after = r > shard
        carried = carried + jnp.where(after, factor, 0.0) * states[r, :state].astype(jnp.float32)
        whole = states[r, state : state + 1].astype(jnp.float32) + states[
            r, state + 1 : state + 2
        ].astype(jnp.float32)
        factor = jnp.where(after, factor * whole, factor)
    cross = tail * mm(b_rows, carried.astype(bf), NN)
    head_grad = (local_part + cross).astype(bf)
    return (head_grad[None], input_grad[None], gate_up[0], gate_up[1], down[0])


def solution(mesh):
    return jax.shard_map(
        body,
        mesh=mesh,
        in_specs=(
            P("seq", "expert", None),
            P("seq", "expert", None),
            P("seq", "expert", None),
            P("expert", None, "seq"),
            P("expert", None, "seq"),
            P("expert", "seq", None),
            P("expert", None),
            P("seq", None, None),
            P("seq", None, None),
            P("seq", "expert", None),
        ),
        out_specs=(
            P("seq", None, "expert"),
            P("seq", "expert", None),
            P("expert", None, "seq"),
            P("expert", None, "seq"),
            P("expert", "seq", None),
        ),
        check_vma=False,
    )
```

```python
import jax
import jax.numpy as jnp
from jax import lax
from jax.experimental import pallas as pl
from jax.experimental.pallas import tpu as pltpu
from jax.sharding import PartitionSpec as P

P_SIZE = 64
CAP = 10
VMEM = 60 * 1024 * 1024
NN = (((1,), (0,)), ((), ()))
NT = (((1,), (1,)), ((), ()))
TN = (((0,), (0,)), ((), ()))


def mm(a, b, dims):
    return lax.dot_general(a, b, dims, preferred_element_type=jnp.float32)


def terms_kernel(x_ref, dy_ref, wg_ref, wu_ref, wd_ref, h_ref, g_ref, u_ref, back_ref, acc):
    step = pl.program_id(0)
    x = x_ref[0]
    gate = mm(x, wg_ref[0], NN)
    up = mm(x, wu_ref[0], NN)
    grad = mm(dy_ref[0], wd_ref[0], NT)
    logistic = jax.nn.sigmoid(gate)
    activated = gate * logistic
    h_ref[...] = (activated * up).astype(jnp.bfloat16)
    up_term = (grad * activated).astype(jnp.bfloat16)
    gate_term = (grad * up * logistic * (1.0 + gate * (1.0 - logistic))).astype(jnp.bfloat16)
    g_ref[...] = gate_term
    u_ref[...] = up_term
    part = mm(gate_term, wg_ref[0], NT) + mm(up_term, wu_ref[0], NT)

    @pl.when(step == 0)
    def _():
        acc[...] = part

    @pl.when(step > 0)
    def _():
        acc[...] += part

    @pl.when(step == pl.num_programs(0) - 1)
    def _():
        back_ref[...] = acc[...].astype(jnp.bfloat16)


def expert_terms(e, local, gathered, w_gate, w_up, w_down):
    rows, width = gathered.shape[1:]
    hidden = w_gate.shape[2]
    tile = min(512, hidden)
    whole = pl.BlockSpec((rows, width), lambda i: (0, 0))
    part = pl.BlockSpec((rows, tile), lambda i: (0, i))
    column = pl.BlockSpec((1, width, tile), lambda i: (e, 0, i))
    row = pl.BlockSpec((1, tile, width), lambda i: (e, i, 0))
    term = jax.ShapeDtypeStruct((rows, hidden), jnp.bfloat16)
    return pl.pallas_call(
        terms_kernel,
        grid=(hidden // tile,),
        in_specs=[
            pl.BlockSpec((1, rows, width), lambda i: (e, 0, 0)),
            pl.BlockSpec((1, rows, width), lambda i: (local + e, 0, 0)),
            column,
            column,
            row,
        ],
        out_specs=[part, part, part, whole],
        out_shape=[term, term, term, jax.ShapeDtypeStruct((rows, width), jnp.bfloat16)],
        scratch_shapes=[pltpu.VMEM((rows, width), jnp.float32)],
        compiler_params=pltpu.CompilerParams(vmem_limit_bytes=VMEM),
        cost_estimate=pl.CostEstimate(
            flops=10 * rows * width * hidden,
            bytes_accessed=6 * width * hidden + 6 * rows * width,
            transcendentals=rows * hidden,
        ),
        name="expert_terms",
    )(gathered, gathered, w_gate, w_up, w_down)


def weight_grads(e, count, left, rights, held):
    left, left_at = left
    rows, width = left.shape[1:]
    breadth = rights[0][0].shape[2]
    tile = min(256, width)
    number = len(rights)

    def kernel(*refs):
        left_ref, right_refs, out_refs = refs[0], refs[1 : 1 + number], refs[-number:]
        for right_ref, out_ref in zip(right_refs, out_refs):
            out_ref[0] = mm(left_ref[0], right_ref[0], TN)

    out = pl.BlockSpec((1, tile, breadth), lambda i: (e, i, 0))
    kept = [] if held is None else list(held)
    return pl.pallas_call(
        kernel,
        grid=(width // tile,),
        in_specs=[pl.BlockSpec((1, rows, tile), lambda i: (left_at, 0, i))]
        + [pl.BlockSpec((1, rows, breadth), lambda i, at=at: (at, 0, 0)) for _, at in rights]
        + [pl.BlockSpec(memory_space=pl.ANY)] * len(kept),
        out_specs=[out] * number,
        out_shape=[jax.ShapeDtypeStruct((count, width, breadth), jnp.float32)] * number,
        input_output_aliases={1 + number + k: k for k in range(len(kept))},
        compiler_params=pltpu.CompilerParams(vmem_limit_bytes=VMEM),
        cost_estimate=pl.CostEstimate(
            flops=2 * number * rows * width * breadth,
            bytes_accessed=4 * number * width * breadth,
            transcendentals=0,
        ),
        name="weight_grads",
    )(left, *[right for right, _ in rights], *kept)


def body(moe_input, out_grad, expert_id, w_gate, w_up, w_down, w_out, b_proj, c_proj, log_decay):
    groups = lax.axis_size("expert")
    group = lax.axis_index("expert")
    shards = lax.axis_size("seq")
    shard = lax.axis_index("seq")
    local = w_gate.shape[0]
    tokens, width = moe_input.shape[1:]
    heads = w_out.shape[0] // P_SIZE
    lanes = heads * P_SIZE
    length, state = b_proj.shape[1:]
    bf = jnp.bfloat16

    def places(labels):
        here = jnp.arange(labels.shape[0], dtype=jnp.int32)
        same = (
            (labels[:, None] == labels[None, :])
            & (here[:, None] // tokens == here[None, :] // tokens)
            & (here[None, :] < here[:, None])
        )
        return (here // tokens) * CAP + jnp.sum(same.astype(jnp.int32), axis=1)

    span = groups * CAP
    kinds = 2 * local
    block = kinds * CAP
    labels = expert_id[0, :, 0]
    sent_row = (labels // local) * block + (labels % local) * CAP + places(labels)
    sent_rows = jnp.concatenate([sent_row, sent_row + local * CAP])
    placing = (
        jnp.arange(groups * block, dtype=jnp.int32)[:, None] == sent_rows[None, :]
    ).astype(bf)
    both = jnp.concatenate([moe_input[0], out_grad[0]], axis=0)
    picked = mm(placing, both, NN).astype(bf)
    received = lax.all_to_all(
        picked.reshape(groups, block, width), "expert", split_axis=0, concat_axis=0, tiled=True
    ).reshape(groups * block, width)
    rank = jnp.arange(groups * block, dtype=jnp.int32)
    source = (rank % span) // CAP * block + rank // span * CAP + rank % CAP
    order = (source[:, None] == rank[None, :]).astype(bf)
    arranged = mm(order, received, NN).astype(bf).reshape(kinds, span, width)
    gathered = lax.all_gather(arranged, "seq", axis=1, tiled=True)

    late = jnp.concatenate(
        [out_grad[0], jnp.broadcast_to(expert_id[0], (tokens, 128)).astype(bf)], axis=1
    )
    gathered, late = lax.optimization_barrier((gathered, late))
    dy_all = lax.all_gather(late, "expert", axis=0, tiled=True)

    terms = [expert_terms(e, local, gathered, w_gate, w_up, w_down) for e in range(local)]
    back = jnp.stack([t[3].reshape(shards, span, width) for t in terms], axis=1)
    summed = lax.psum_scatter(
        back.reshape(shards, local * span, width), "seq", scatter_dimension=0, tiled=True
    )[0]
    gate_up, down = None, None
    for e in range(local):
        hidden, gate_term, up_term, _ = terms[e]
        gate_up = weight_grads(
            e, local, (gathered, e), [(gate_term[None], 0), (up_term[None], 0)], gate_up
        )
        down = weight_grads(e, local, (hidden[None], 0), [(gathered, local + e)], down)

    here = jnp.arange(length, dtype=jnp.int32)
    labels = dy_all[:, width].astype(jnp.int32)
    place = places(labels)
    acum = jnp.cumsum(log_decay[0], axis=1)
    b_rows, c_rows = b_proj[0], c_proj[0]
    wide = jnp.repeat(acum.T, P_SIZE, axis=1)
    grow = jnp.exp(wide)
    tail = jnp.exp(wide[-1:] - wide)
    total = grow[-1:]
    high = total.astype(bf)
    low = (total - high.astype(jnp.float32)).astype(bf)
    later = here[:, None] >= here[None, :]
    scores = jnp.where(later, mm(c_rows, b_rows, NT), 0.0)
    difference = jnp.where(later[None], acum[:, :, None] - acum[:, None, :], 0.0)
    weight = (jnp.exp(difference) * scores[None]).astype(bf)
    head_base = mm(dy_all[:, :width], w_out, NT)
    summed, gate_up, down, head_base, weight, grow, tail = lax.optimization_barrier(
        (summed, gate_up, down, head_base, weight, grow, tail)
    )
    returned = lax.all_gather(summed, "expert", axis=0, tiled=True)
    row = (labels // local) * (local * span) + (labels % local) * span + place
    take = (row[:, None] == jnp.arange(groups * local * span, dtype=jnp.int32)[None, :]).astype(bf)
    expert_all = mm(take, returned, NN)
    expert_all = expert_all.astype(bf)
    own = lax.dynamic_slice_in_dim(expert_all, group * tokens, tokens, axis=0)
    input_grad = (out_grad[0].astype(jnp.float32) + own.astype(jnp.float32)).astype(bf)

    head_out = head_base + mm(expert_all, w_out, NT)
    summary = mm(c_rows, (grow * head_out).astype(bf), TN).astype(bf)
    sent = jnp.concatenate([summary, high, low, jnp.zeros((14, lanes), bf)], axis=0)
    states = lax.all_to_all(sent, "seq", split_axis=1, concat_axis=0, tiled=True)
    states = states.reshape(shards, state + 16, lanes // shards).astype(jnp.float32)
    local_part = jnp.einsum(
        "hts,thp->shp",
        weight,
        head_out.astype(bf).reshape(length, heads, P_SIZE),
        preferred_element_type=jnp.float32,
    ).reshape(length, lanes)
    carry = jnp.zeros((state, lanes // shards), jnp.float32)
    carries = [carry]
    for r in range(shards - 1, 0, -1):
        whole = states[r, state : state + 1] + states[r, state + 1 : state + 2]
        carry = states[r, :state] + whole * carry
        carries.append(carry)
    carries = jnp.concatenate(carries[::-1], axis=0).astype(bf)
    carried = lax.all_to_all(carries, "seq", split_axis=0, concat_axis=1, tiled=True)
    cross = tail * mm(b_rows, carried, NN)
    head_grad = (local_part + cross).astype(bf)
    return (head_grad[None], input_grad[None], gate_up[0], gate_up[1], down[0])


def solution(mesh):
    return jax.shard_map(
        body,
        mesh=mesh,
        in_specs=(
            P("seq", "expert", None),
            P("seq", "expert", None),
            P("seq", "expert", None),
            P("expert", None, "seq"),
            P("expert", None, "seq"),
            P("expert", "seq", None),
            P("expert", None),
            P("seq", None, None),
            P("seq", None, None),
            P("seq", "expert", None),
        ),
        out_specs=(
            P("seq", None, "expert"),
            P("seq", "expert", None),
            P("expert", None, "seq"),
            P("expert", None, "seq"),
            P("expert", "seq", None),
        ),
        check_vma=False,
    )
```

```python
import jax
import jax.numpy as jnp
from jax import lax
from jax.experimental import pallas as pl
from jax.experimental.pallas import tpu as pltpu
from jax.sharding import PartitionSpec as P

P_SIZE = 64
CAP = 10
VMEM = 60 * 1024 * 1024
NN = (((1,), (0,)), ((), ()))
NT = (((1,), (1,)), ((), ()))
TN = (((0,), (0,)), ((), ()))


def mm(a, b, dims):
    return lax.dot_general(a, b, dims, preferred_element_type=jnp.float32)


def terms_kernel(x_ref, dy_ref, wg_ref, wu_ref, wd_ref, h_ref, g_ref, u_ref, back_ref, acc):
    step = pl.program_id(0)
    x = x_ref[0]
    gate = mm(x, wg_ref[0], NN)
    up = mm(x, wu_ref[0], NN)
    grad = mm(dy_ref[0], wd_ref[0], NT)
    logistic = jax.nn.sigmoid(gate)
    activated = gate * logistic
    h_ref[...] = (activated * up).astype(jnp.bfloat16)
    up_term = (grad * activated).astype(jnp.bfloat16)
    gate_term = (grad * up * logistic * (1.0 + gate * (1.0 - logistic))).astype(jnp.bfloat16)
    g_ref[...] = gate_term
    u_ref[...] = up_term
    part = mm(gate_term, wg_ref[0], NT) + mm(up_term, wu_ref[0], NT)

    @pl.when(step == 0)
    def _():
        acc[...] = part

    @pl.when(step > 0)
    def _():
        acc[...] += part

    @pl.when(step == pl.num_programs(0) - 1)
    def _():
        back_ref[...] = acc[...].astype(jnp.bfloat16)


def expert_terms(e, local, gathered, w_gate, w_up, w_down):
    rows, width = gathered.shape[1:]
    hidden = w_gate.shape[2]
    tile = min(512, hidden)
    whole = pl.BlockSpec((rows, width), lambda i: (0, 0))
    part = pl.BlockSpec((rows, tile), lambda i: (0, i))
    column = pl.BlockSpec((1, width, tile), lambda i: (e, 0, i))
    row = pl.BlockSpec((1, tile, width), lambda i: (e, i, 0))
    term = jax.ShapeDtypeStruct((rows, hidden), jnp.bfloat16)
    return pl.pallas_call(
        terms_kernel,
        grid=(hidden // tile,),
        in_specs=[
            pl.BlockSpec((1, rows, width), lambda i: (e, 0, 0)),
            pl.BlockSpec((1, rows, width), lambda i: (local + e, 0, 0)),
            column,
            column,
            row,
        ],
        out_specs=[part, part, part, whole],
        out_shape=[term, term, term, jax.ShapeDtypeStruct((rows, width), jnp.bfloat16)],
        scratch_shapes=[pltpu.VMEM((rows, width), jnp.float32)],
        compiler_params=pltpu.CompilerParams(vmem_limit_bytes=VMEM),
        cost_estimate=pl.CostEstimate(
            flops=10 * rows * width * hidden,
            bytes_accessed=6 * width * hidden + 6 * rows * width,
            transcendentals=rows * hidden,
        ),
        name="expert_terms",
    )(gathered, gathered, w_gate, w_up, w_down)


def weight_grads(e, count, left, rights, held):
    left, left_at = left
    rows, width = left.shape[1:]
    breadth = rights[0][0].shape[2]
    tile = min(256, width)
    number = len(rights)

    def kernel(*refs):
        left_ref, right_refs, out_refs = refs[0], refs[1 : 1 + number], refs[-number:]
        for right_ref, out_ref in zip(right_refs, out_refs):
            out_ref[0] = mm(left_ref[0], right_ref[0], TN)

    out = pl.BlockSpec((1, tile, breadth), lambda i: (e, i, 0))
    kept = [] if held is None else list(held)
    return pl.pallas_call(
        kernel,
        grid=(width // tile,),
        in_specs=[pl.BlockSpec((1, rows, tile), lambda i: (left_at, 0, i))]
        + [pl.BlockSpec((1, rows, breadth), lambda i, at=at: (at, 0, 0)) for _, at in rights]
        + [pl.BlockSpec(memory_space=pl.ANY)] * len(kept),
        out_specs=[out] * number,
        out_shape=[jax.ShapeDtypeStruct((count, width, breadth), jnp.float32)] * number,
        input_output_aliases={1 + number + k: k for k in range(len(kept))},
        compiler_params=pltpu.CompilerParams(vmem_limit_bytes=VMEM),
        cost_estimate=pl.CostEstimate(
            flops=2 * number * rows * width * breadth,
            bytes_accessed=4 * number * width * breadth,
            transcendentals=0,
        ),
        name="weight_grads",
    )(left, *[right for right, _ in rights], *kept)


def body(moe_input, out_grad, expert_id, w_gate, w_up, w_down, w_out, b_proj, c_proj, log_decay):
    groups = lax.axis_size("expert")
    group = lax.axis_index("expert")
    shards = lax.axis_size("seq")
    shard = lax.axis_index("seq")
    local = w_gate.shape[0]
    tokens, width = moe_input.shape[1:]
    heads = w_out.shape[0] // P_SIZE
    lanes = heads * P_SIZE
    length, state = b_proj.shape[1:]
    bf = jnp.bfloat16

    def places(labels):
        here = jnp.arange(labels.shape[0], dtype=jnp.int32)
        same = (
            (labels[:, None] == labels[None, :])
            & (here[:, None] // tokens == here[None, :] // tokens)
            & (here[None, :] < here[:, None])
        )
        return (here // tokens) * CAP + jnp.sum(same.astype(jnp.int32), axis=1)

    span = groups * CAP
    kinds = 2 * local
    block = kinds * CAP
    labels = expert_id[0, :, 0]
    sent_row = (labels // local) * block + (labels % local) * CAP + places(labels)
    sent_rows = jnp.concatenate([sent_row, sent_row + local * CAP])
    placing = (
        jnp.arange(groups * block, dtype=jnp.int32)[:, None] == sent_rows[None, :]
    ).astype(bf)
    both = jnp.concatenate([moe_input[0], out_grad[0]], axis=0)
    picked = mm(placing, both, NN).astype(bf)
    received = lax.all_to_all(
        picked.reshape(groups, block, width), "expert", split_axis=0, concat_axis=0, tiled=True
    ).reshape(groups * block, width)
    rank = jnp.arange(groups * block, dtype=jnp.int32)
    source = (rank % span) // CAP * block + rank // span * CAP + rank % CAP
    order = (source[:, None] == rank[None, :]).astype(bf)
    arranged = mm(order, received, NN).astype(bf).reshape(kinds, span, width)
    gathered = lax.all_gather(arranged, "seq", axis=1, tiled=True)

    late = jnp.concatenate(
        [out_grad[0], jnp.broadcast_to(expert_id[0], (tokens, 128)).astype(bf)], axis=1
    )
    gathered, late = lax.optimization_barrier((gathered, late))
    dy_all = lax.all_gather(late, "expert", axis=0, tiled=True)

    terms = [expert_terms(e, local, gathered, w_gate, w_up, w_down) for e in range(local)]
    back = jnp.stack([t[3].reshape(shards, span, width) for t in terms], axis=1)
    summed = lax.psum_scatter(
        back.reshape(shards, local * span, width), "seq", scatter_dimension=0, tiled=True
    )[0]
    gate_up, down = None, None
    for e in range(local):
        hidden, gate_term, up_term, _ = terms[e]
        gate_up = weight_grads(
            e, local, (gathered, e), [(gate_term[None], 0), (up_term[None], 0)], gate_up
        )
        down = weight_grads(e, local, (hidden[None], 0), [(gathered, local + e)], down)

    here = jnp.arange(length, dtype=jnp.int32)
    labels = dy_all[:, width].astype(jnp.int32)
    place = places(labels)
    acum = jnp.cumsum(log_decay[0], axis=1)
    b_rows, c_rows = b_proj[0], c_proj[0]
    wide = jnp.repeat(acum.T, P_SIZE, axis=1)
    grow = jnp.exp(wide)
    tail = jnp.exp(wide[-1:] - wide)
    total = grow[-1:]
    high = total.astype(bf)
    low = (total - high.astype(jnp.float32)).astype(bf)
    later = here[:, None] >= here[None, :]
    scores = jnp.where(later, mm(c_rows, b_rows, NT), 0.0)
    difference = jnp.where(later[None], acum[:, :, None] - acum[:, None, :], 0.0)
    weight = (jnp.exp(difference) * scores[None]).astype(bf)
    head_base = mm(dy_all[:, :width], w_out, NT)
    summed, gate_up, down, head_base, weight, grow, tail = lax.optimization_barrier(
        (summed, gate_up, down, head_base, weight, grow, tail)
    )
    returned = jnp.concatenate(
        [summed]
        + [
            lax.ppermute(summed, "expert", [(i, (i + k) % groups) for i in range(groups)])
            for k in range(1, groups)
        ],
        axis=0,
    )
    behind = (group - labels // local + groups) % groups
    row = behind * (local * span) + (labels % local) * span + place
    take = (row[:, None] == jnp.arange(groups * local * span, dtype=jnp.int32)[None, :]).astype(bf)
    expert_all = mm(take, returned, NN)
    expert_all = expert_all.astype(bf)
    own = lax.dynamic_slice_in_dim(expert_all, group * tokens, tokens, axis=0)
    input_grad = (out_grad[0].astype(jnp.float32) + own.astype(jnp.float32)).astype(bf)

    head_out = head_base + mm(expert_all, w_out, NT)
    summary = mm(c_rows, (grow * head_out).astype(bf), TN).astype(bf)
    sent = jnp.concatenate([summary, high, low, jnp.zeros((14, lanes), bf)], axis=0)
    states = lax.all_to_all(sent, "seq", split_axis=1, concat_axis=0, tiled=True)
    states = states.reshape(shards, state + 16, lanes // shards).astype(jnp.float32)
    local_part = jnp.einsum(
        "hts,thp->shp",
        weight,
        head_out.astype(bf).reshape(length, heads, P_SIZE),
        preferred_element_type=jnp.float32,
    ).reshape(length, lanes)
    carry = jnp.zeros((state, lanes // shards), jnp.float32)
    carries = [carry]
    for r in range(shards - 1, 0, -1):
        whole = states[r, state : state + 1] + states[r, state + 1 : state + 2]
        carry = states[r, :state] + whole * carry
        carries.append(carry)
    carries = jnp.concatenate(carries[::-1], axis=0).astype(bf)
    carried = lax.all_to_all(carries, "seq", split_axis=0, concat_axis=1, tiled=True)
    cross = tail * mm(b_rows, carried, NN)
    head_grad = (local_part + cross).astype(bf)
    return (head_grad[None], input_grad[None], gate_up[0], gate_up[1], down[0])


def solution(mesh):
    return jax.shard_map(
        body,
        mesh=mesh,
        in_specs=(
            P("seq", "expert", None),
            P("seq", "expert", None),
            P("seq", "expert", None),
            P("expert", None, "seq"),
            P("expert", None, "seq"),
            P("expert", "seq", None),
            P("expert", None),
            P("seq", None, None),
            P("seq", None, None),
            P("seq", "expert", None),
        ),
        out_specs=(
            P("seq", None, "expert"),
            P("seq", "expert", None),
            P("expert", None, "seq"),
            P("expert", None, "seq"),
            P("expert", "seq", None),
        ),
        check_vma=False,
    )
```
